512 devices in a mesh: seq: 64 (over z, y), head: 8 (over x, core).
Axes of the slice: x: 4, y: 8, z: 8, core: 2. Of those that a mesh axis runs over, the one named last changes fastest.
Arguments:
- query_rows: bfloat16 [16, 16384, 128], P('head', 'seq'), may hold values from -6 to 6
- key_rows: bfloat16 [16, 16384, 128], P('head', 'seq'), may hold values from -6 to 6
- value_rows: bfloat16 [16, 16384, 128], P('head', 'seq'), may hold values from -6 to 6
- norm_gain: float32 [16, 128], P('head'), may hold values from 0.25 to 1.75
- level_table: float32 [16, 16, 6], P(None, 'head'), may hold values from 0.3 to 4.5
- level_index: int32 [16384, 6], P('seq'), may hold values from 0 to 15
- window_length: int32 [16], P('head'), may hold values from 512 to 1024, as said below
- out_grad: bfloat16 [16, 16384, 128], P('head', 'seq'), may hold values from -18 to 18
Outputs:
- layer_out: bfloat16 [16, 16384, 128], P('head', 'seq')
- query_grad: bfloat16 [16, 16384, 128], P('head', 'seq')
- key_grad: bfloat16 [16, 16384, 128], P('head', 'seq')
- value_grad: bfloat16 [16, 16384, 128], P('head', 'seq')
- table_grad: float32 [16, 16, 6], P(None, 'head')
- gain_grad: float32 [16, 128], P('head')
The draws below stay inside these ranges and needn't reach their ends.
Inputs may be any that keep to these rules, and one draw needn't show every extreme that they name: `window_length`: every head's window holds at least half of 1024 tokens and at most 1024; some head's window is exactly 1024.
All inputs are finite; a program needn't handle non-finite values.
Results may differ from the reference program's by a relative error of at most 0.0078.
Values may be sent and summed in bfloat16 or wider, within the bound.
A program may use at most 64 MiB of HBM per device.

```python
import math
import jax
import jax.numpy as jnp
from jax import lax

H = 16
HD = 128
BLOCK = 64
WINDOW = 1024
LEVELS = 6
TABLE_ROWS = 16
TOKENS = 16384


def draw_level_table(key, part):
    ramp = 1.0 + 2.0 * jnp.arange(H, dtype=jnp.float32) / (H - 1)
    base = jnp.exp(jax.random.uniform(key, (TABLE_ROWS, H, LEVELS), jnp.float32, math.log(0.3), math.log(1.5)))
    return base * ramp[None, :, None]


def draw_window_length(key, part):
    lengths = jax.random.randint(jax.random.fold_in(key, 11), (H,), WINDOW // 2, WINDOW + 1, dtype=jnp.int32)
    chosen = jax.random.randint(jax.random.fold_in(key, 12), (), 0, H, dtype=jnp.int32)
    return jnp.where(jnp.arange(H, dtype=jnp.int32) == chosen, WINDOW, lengths).astype(jnp.int32)


def draw_out_grad(key, part):
    ramp = 1.0 + 2.0 * jnp.arange(TOKENS, dtype=jnp.float32) / (TOKENS - 1)
    base = jnp.clip(jax.random.normal(key, (H, TOKENS, HD), jnp.float32), -6.0, 6.0)
    return (base * ramp[None, :, None]).astype(jnp.bfloat16)


def place_ends(result, rng, smallest, high):
    index_at = [jax.random.randint(jax.random.fold_in(rng, axis), (), 0, length) for axis, length in enumerate(result.shape)]
    main_axis = result.shape.index(max(result.shape))
    beside = index_at[:main_axis] + [(index_at[main_axis] + 1) % result.shape[main_axis]] + index_at[main_axis + 1:]
    return result.at[tuple(index_at)].set(smallest).at[tuple(beside)].set(high)


def levels(key, dims, split, smallest, high):
    gain = 1.0
    for dim, blocks in split:
        steps = jax.random.uniform(jax.random.fold_in(jax.random.fold_in(key, 6), dim), (blocks,), jnp.float32, smallest / len(split), high / len(split))
        gain = gain * jnp.repeat(jnp.exp(steps), dims[dim] // blocks).reshape((-1,) + (1,) * (len(dims) - 1 - dim))
    return gain


def bell_draw(rng, extent, deviation, limit, cuts=(), kind=jnp.bfloat16):
    entries = jax.random.normal(rng, extent, jnp.float32) * deviation
    if len(cuts) > 0:
        entries = levels(rng, extent, cuts, -0.22, 0.18) * entries
    return jnp.clip(entries, min=-limit, max=limit).astype(kind)


def setup_inputs(seed: int = 0) -> dict:
    streams_of = jax.random.split(jax.random.key(seed), 9)
    query_rows = bell_draw(streams_of[0], (H, TOKENS, HD), 1.0, 6.0, ((0, 8), (1, 64)))
    key_rows = bell_draw(streams_of[1], (H, TOKENS, HD), 1.0, 6.0, ((0, 8), (1, 64)))
    value_rows = bell_draw(streams_of[2], (H, TOKENS, HD), 1.0, 6.0, ((0, 8), (1, 64)))
    norm_gain = jnp.clip(1.0 + 0.15 * jax.random.normal(streams_of[3], (H, HD), jnp.float32), 0.25, 1.75)
    level_table = draw_level_table(jax.random.fold_in(streams_of[8], 71), 0)
    level_index = place_ends(jax.random.randint(streams_of[5], (TOKENS, LEVELS), 0, TABLE_ROWS), jax.random.fold_in(streams_of[5], 1), 0, TABLE_ROWS - 1).astype(jnp.int32)
    window_length = draw_window_length(jax.random.fold_in(streams_of[8], 71), 0)
    out_grad = draw_out_grad(jax.random.fold_in(streams_of[8], 71), 0)
    return {"query_rows": query_rows, "key_rows": key_rows, "value_rows": value_rows, "norm_gain": norm_gain, "level_table": level_table, "level_index": level_index, "window_length": window_length, "out_grad": out_grad}


epsilon = 1e-06
block_cap = 512

def product(pattern, left_side, right_side):
    return jnp.einsum(pattern, left_side.astype(jnp.float32), right_side.astype(jnp.float32), precision=lax.Precision.HIGHEST)

def causal_mask():
    row_pos = lax.broadcasted_iota(jnp.int32, (BLOCK, BLOCK), 0)
    col_pos = lax.broadcasted_iota(jnp.int32, (BLOCK, BLOCK), 1)
    return row_pos >= col_pos

def window_mask(block_rows, span_len):
    query_pos = lax.broadcasted_iota(jnp.int32, (1, block_rows, WINDOW + block_rows), 1)
    key_pos = lax.broadcasted_iota(jnp.int32, (1, block_rows, WINDOW + block_rows), 2)
    offset = query_pos + WINDOW - key_pos
    return (offset >= 0) & (offset < span_len[:, None, None])

def leaf_view(tensor):
    head_count, token_count, head_dim = tensor.shape
    return tensor.reshape(head_count, token_count // BLOCK, BLOCK, head_dim)

def split_level(tensor, group_len):
    head_count, token_count, head_dim = tensor.shape
    return tensor.reshape(head_count, token_count // (2 * group_len), 2, group_len, head_dim)

def level_summary(key_rows, value_rows, group_len):
    lower_sum = product('hpse,hpsf->hpef', split_level(key_rows, group_len)[:, :, 0], split_level(value_rows, group_len)[:, :, 0])
    return (lower_sum * (1.0 / math.sqrt(group_len * key_rows.shape[-1]))).astype(jnp.bfloat16)

def level_area(query_rows, summary, group_len):
    upper_half = product('hpse,hpef->hpsf', split_level(query_rows, group_len)[:, :, 1], summary)
    return jnp.stack([jnp.zeros_like(upper_half), upper_half], axis=2).reshape(query_rows.shape)

def level_grads(query_rows, key_rows, value_rows, summary, upstream, group_len):
    upstream_up = split_level(upstream, group_len)[:, :, 1]
    query_up = product('hpsf,hpef->hpse', upstream_up, summary)
    summary_grad = product('hpse,hpsf->hpef', split_level(query_rows, group_len)[:, :, 1], upstream_up)
    low_grad = (summary_grad * (1.0 / math.sqrt(group_len * query_rows.shape[-1]))).astype(jnp.bfloat16)
    key_low = product('hpsf,hpef->hpse', split_level(value_rows, group_len)[:, :, 0], low_grad)
    value_low = product('hpse,hpef->hpsf', split_level(key_rows, group_len)[:, :, 0], low_grad)
    blank = jnp.zeros_like(query_up)
    full_shape = query_rows.shape
    return (jnp.stack([blank, query_up], axis=2).reshape(full_shape), jnp.stack([key_low, blank], axis=2).reshape(full_shape), jnp.stack([value_low, blank], axis=2).reshape(full_shape))

def window_setup(query_rows, key_rows, value_rows, window_length):
    head_count, token_count, head_dim = query_rows.shape
    block_rows = min(block_cap, token_count)
    padding = jnp.zeros((head_count, WINDOW, head_dim), jnp.bfloat16)
    key_pad = jnp.concatenate([padding, key_rows], axis=1)
    value_pad = jnp.concatenate([padding, value_rows], axis=1)
    score_scale = lax.rsqrt((head_dim * window_length).astype(jnp.float32))[:, None, None]
    inside = window_mask(block_rows, window_length)
    return (block_rows, key_pad, value_pad, score_scale, inside)

def window_forward(query_rows, key_rows, value_rows, window_length):
    token_count = query_rows.shape[1]
    block_rows, key_pad, value_pad, score_scale, inside = window_setup(query_rows, key_rows, value_rows, window_length)

    def one_block(block_no):
        row_start = block_no * block_rows
        query_part = lax.dynamic_slice_in_dim(query_rows, row_start, block_rows, 1)
        key_part = lax.dynamic_slice_in_dim(key_pad, row_start, WINDOW + block_rows, 1)
        value_part = lax.dynamic_slice_in_dim(value_pad, row_start, WINDOW + block_rows, 1)
        prob_low = jnp.where(inside, product('hqe,hke->hqk', query_part, key_part) * score_scale, 0.0).astype(jnp.bfloat16)
        return product('hqk,hke->hqe', prob_low, value_part)
    blocks = lax.map(one_block, jnp.arange(token_count // block_rows, dtype=jnp.int32))
    return jnp.transpose(blocks, (1, 0, 2, 3)).reshape(query_rows.shape)

def window_backward(query_rows, key_rows, value_rows, grad_low, window_length):
    head_count, token_count, head_dim = query_rows.shape
    block_rows, key_pad, value_pad, score_scale, inside = window_setup(query_rows, key_rows, value_rows, window_length)

    def one_block(pending, block_no):
        key_acc, value_acc = pending
        row_start = block_no * block_rows
        query_part = lax.dynamic_slice_in_dim(query_rows, row_start, block_rows, 1)
        grad_part = lax.dynamic_slice_in_dim(grad_low, row_start, block_rows, 1)
        key_part = lax.dynamic_slice_in_dim(key_pad, row_start, WINDOW + block_rows, 1)
        value_part = lax.dynamic_slice_in_dim(value_pad, row_start, WINDOW + block_rows, 1)
        prob_low = jnp.where(inside, product('hqe,hke->hqk', query_part, key_part) * score_scale, 0.0).astype(jnp.bfloat16)
        prob_grad = product('hqe,hke->hqk', grad_part, value_part)
        score_grad = jnp.where(inside, prob_grad * score_scale, 0.0).astype(jnp.bfloat16)
        query_part_grad = product('hqk,hke->hqe', score_grad, key_part)
        key_new = lax.dynamic_slice_in_dim(key_acc, row_start, WINDOW + block_rows, 1) + product('hqk,hqe->hke', score_grad, query_part)
        value_new = lax.dynamic_slice_in_dim(value_acc, row_start, WINDOW + block_rows, 1) + product('hqk,hqe->hke', prob_low, grad_part)
        anchor = jnp.zeros((), jnp.int32)
        key_acc = lax.dynamic_update_slice(key_acc, key_new, (anchor, row_start, anchor))
        value_acc = lax.dynamic_update_slice(value_acc, value_new, (anchor, row_start, anchor))
        return ((key_acc, value_acc), query_part_grad)
    start_acc = jnp.zeros((head_count, WINDOW + token_count, head_dim), jnp.float32)
    (key_acc, value_acc), blocks = lax.scan(one_block, (start_acc, start_acc), jnp.arange(token_count // block_rows, dtype=jnp.int32))
    query_grad = jnp.transpose(blocks, (1, 0, 2, 3)).reshape(query_rows.shape)
    return (query_grad, key_acc[:, WINDOW:], value_acc[:, WINDOW:])

def reference(query_rows, key_rows, value_rows, norm_gain, level_table, level_index, window_length, out_grad):
    head_count, token_count, head_dim = query_rows.shape
    top_level = (token_count // BLOCK).bit_length() - 1
    onehot = (level_index[:, :, None] == jnp.arange(TABLE_ROWS, dtype=jnp.int32)[None, None, :]).astype(jnp.float32)
    weights = jnp.einsum('tjk,khj->htj', onehot, level_table, precision=lax.Precision.HIGHEST)

    def weight_of(level_no):
        return weights[:, :, min(level_no, LEVELS - 1)][:, :, None]
    query_leaf = leaf_view(query_rows)
    key_leaf = leaf_view(key_rows)
    value_leaf = leaf_view(value_rows)
    leaf_scale = 1.0 / math.sqrt(BLOCK * head_dim)
    causal = causal_mask()
    leaf_prob = jnp.where(causal, product('hcte,hcse->hcts', query_leaf, key_leaf) * leaf_scale, 0.0).astype(jnp.bfloat16)
    leaf_area = product('hcts,hcse->hcte', leaf_prob, value_leaf).reshape(query_rows.shape)
    mixed = window_forward(query_rows, key_rows, value_rows, window_length) + weight_of(0) * leaf_area
    for level_no in range(1, top_level + 1):
        group_len = BLOCK * 2 ** (level_no - 1)
        summary = level_summary(key_rows, value_rows, group_len)
        mixed = mixed + weight_of(level_no) * level_area(query_rows, summary, group_len)
    inv_rms = lax.rsqrt(lax.optimization_barrier(jnp.sum(mixed * mixed, axis=(0, 2))) / (head_count * head_dim) + epsilon)
    layer_out = (mixed * inv_rms[None, :, None] * norm_gain[:, None, :]).astype(jnp.bfloat16)
    grad_full = out_grad.astype(jnp.float32)
    scaled = grad_full * norm_gain[:, None, :]
    cross_sum = lax.optimization_barrier(jnp.sum(scaled * mixed, axis=(0, 2)))
    mixed_grad = scaled * inv_rms[None, :, None] - mixed * (inv_rms ** 3 * cross_sum / (head_count * head_dim))[None, :, None]
    gain_grad = lax.optimization_barrier(jnp.sum(grad_full * mixed * inv_rms[None, :, None], axis=1))
    grad_low = mixed_grad.astype(jnp.bfloat16)
    columns = [jnp.zeros((head_count, token_count), jnp.float32) for column_no in range(LEVELS)]
    columns[0] = columns[0] + lax.optimization_barrier(jnp.sum(mixed_grad * leaf_area, axis=2))
    upstream_leaf = leaf_view((weight_of(0) * mixed_grad).astype(jnp.bfloat16))
    prob_grad = product('hcte,hcse->hcts', upstream_leaf, value_leaf)
    score_grad = jnp.where(causal, prob_grad * leaf_scale, 0.0).astype(jnp.bfloat16)
    query_grad = product('hcts,hcse->hcte', score_grad, key_leaf).reshape(query_rows.shape)
    key_grad = product('hcts,hcte->hcse', score_grad, query_leaf).reshape(query_rows.shape)
    value_grad = product('hcts,hcte->hcse', leaf_prob, upstream_leaf).reshape(query_rows.shape)
    window_query, window_key, window_value = window_backward(query_rows, key_rows, value_rows, grad_low, window_length)
    query_grad = query_grad + window_query
    key_grad = key_grad + window_key
    value_grad = value_grad + window_value
    for level_no in range(1, top_level + 1):
        group_len = BLOCK * 2 ** (level_no - 1)
        summary = level_summary(key_rows, value_rows, group_len)
        area_now = level_area(query_rows, summary, group_len)
        column_no = min(level_no, LEVELS - 1)
        columns[column_no] = columns[column_no] + lax.optimization_barrier(jnp.sum(mixed_grad * area_now, axis=2))
        upstream = (weight_of(level_no) * mixed_grad).astype(jnp.bfloat16)
        query_part, key_part, value_part = level_grads(query_rows, key_rows, value_rows, summary, upstream, group_len)
        query_grad = query_grad + query_part
        key_grad = key_grad + key_part
        value_grad = value_grad + value_part
    weight_grad = jnp.stack(columns, axis=-1)
    table_grad = jnp.einsum('tjk,htj->khj', onehot, weight_grad, precision=lax.Precision.HIGHEST)
    return (layer_out, query_grad.astype(jnp.bfloat16), key_grad.astype(jnp.bfloat16), value_grad.astype(jnp.bfloat16), table_grad, gain_grad)
```

```python
import functools
import math

import jax
import jax.numpy as jnp
from jax import lax
from jax.experimental import pallas as pl
from jax.experimental.pallas import tpu as pltpu
from jax.sharding import Mesh
from jax.sharding import PartitionSpec as P

BLOCK = 64
LEVELS = 6
ROWS = 16
REACH = 4
HEADS = 2
T = 256
D = 128
RING = 8
PIECE = D // RING
EPS = 1e-06
BF = jnp.bfloat16
F32 = jnp.float32
HIGH = lax.Precision.HIGHEST
MESH = pl.DeviceIdType.MESH


def level_scale(group_len):
    return 1.0 / math.sqrt(group_len * D)


def nn(a, b):
    return lax.dot_general(a, b, (((1,), (0,)), ((), ())), preferred_element_type=F32)


def nt(a, b, precision=None):
    return lax.dot_general(
        a, b, (((1,), (1,)), ((), ())), precision=precision, preferred_element_type=F32
    )


def tn(a, b, precision=None):
    return lax.dot_general(
        a, b, (((0,), (0,)), ((), ())), precision=precision, preferred_element_type=F32
    )


def iota(shape, dim):
    return lax.broadcasted_iota(jnp.int32, shape, dim)


def kernel(
    dims,
    q_in,
    k_in,
    v_in,
    g_in,
    gain,
    table,
    index,
    window,
    out,
    dq_out,
    dk_out,
    dv_out,
    table_out,
    gain_out,
    own,
    kv,
    qs,
    ds,
    ws,
    w_own,
    w_wide,
    w_far,
    p_raw,
    a_mix,
    p_low,
    p_far,
    s_near,
    mix,
    dm,
    rs_send,
    rs_recv,
    z_send,
    z_recv,
    ag_send,
    ag_recv,
    n_send,
    n_recv,
    r_send,
    r_recv,
    in_sem,
    kv_ss,
    kv_rs,
    q_ss,
    q_rs,
    d_ss,
    d_rs,
    w_ss,
    w_rs,
    f_ss,
    f_rs,
    n_ss,
    n_rs,
    r_ss,
    r_rs,
):
    nz, ny, nh = dims
    z = lax.axis_index("seq_0")
    y = lax.axis_index("seq_1")
    hd = lax.axis_index("head")
    s = z * ny + y
    shard_count = nz * ny

    def y_peer(d):
        return (z, lax.rem(y + d, ny), hd)

    def z_peer(d):
        return (lax.rem(z + d, nz), y, hd)

    def h_peer(d):
        return (z, y, lax.rem(hd + d, nh))

    def s_peer(d):
        to = lax.rem(s + d + shard_count, shard_count)
        return (lax.div(to, ny), lax.rem(to, ny), hd)

    def remote(src, dst, ss, rs, to):
        return pltpu.make_async_remote_copy(
            src_ref=src, dst_ref=dst, send_sem=ss, recv_sem=rs, device_id=to, device_id_type=MESH
        )

    sent = []

    def go(copy):
        copy.start()
        sent.append(copy)
        return copy

    barrier = pltpu.get_barrier_semaphore()
    peers = [s_peer(1), s_peer(-1)]
    peers += [y_peer(d) for d in range(1, ny)]
    peers += [z_peer(d) for d in range(1, nz)]
    peers += [h_peer(d) for d in range(1, nh)]
    for peer in peers:
        pl.semaphore_signal(barrier, inc=1, device_id=peer, device_id_type=MESH)

    loads = []
    for n, ref in enumerate((k_in, v_in, q_in, g_in)):
        load = pltpu.make_async_copy(ref, own.at[n], in_sem.at[n])
        load.start()
        loads.append(load)
    loads[0].wait()
    loads[1].wait()
    K, V, Q, G = 0, 1, 2, 3

    for h in range(HEADS):
        state = tn(own[K, h], own[V, h])
        rs_send[0, :, h] = state.astype(BF).reshape(RING, PIECE, D)

    pl.semaphore_wait(barrier, len(peers))

    def scatter_start(side):
        copies = []
        for d in range(1, ny):
            to = lax.rem(y + d, ny)
            copies.append(
                go(
                    remote(
                        rs_send.at[side, to],
                        rs_recv.at[side, y],
                        f_ss.at[side, 0, d],
                        f_rs.at[side, 0, d],
                        y_peer(d),
                    )
                )
            )
        rs_recv[side, pl.ds(y, 1)] = rs_send[side, pl.ds(y, 1)]
        return copies

    def across_start(side, scattered):
        for copy in scattered:
            copy.wait_recv()
        half = RING // 2
        pieces = [rs_recv[side, n].astype(F32) for n in range(RING)]
        low = functools.reduce(jnp.add, pieces[:half])
        upper = functools.reduce(jnp.add, pieces[half:])
        z_send[side] = (low + upper).astype(BF)
        copies = []
        for d in range(1, nz):
            copies.append(
                go(
                    remote(
                        z_send.at[side],
                        z_recv.at[side, d],
                        f_ss.at[side, 1, d],
                        f_rs.at[side, 1, d],
                        z_peer(d),
                    )
                )
            )
        return copies, (low if side == 0 else upper)

    def gather_start(side, across, near):
        total = jnp.zeros((HEADS, PIECE, D), F32)
        for d in range(1, nz):
            across[d - 1].wait_recv()
            other = lax.rem(z - d + nz, nz)
            counts = (other < z) if side == 0 else (other > z)
            scale = jnp.where(
                lax.div(other, 2) == lax.div(z, 2),
                level_scale(T * 8),
                jnp.where(
                    lax.div(other, 4) == lax.div(z, 4), level_scale(T * 16), level_scale(T * 32)
                ),
            )
            scale = jnp.where(counts, scale, 0.0)
            total = total + z_recv[side, d].astype(F32) * scale
        with_near = (total + near * level_scale(T * 4)).astype(BF)
        plain = total.astype(BF)
        ag_send[side, 0] = plain if side == 0 else with_near
        ag_send[side, 1] = with_near if side == 0 else plain
        copies = []
        for d in range(1, ny):
            to = lax.rem(y + d, ny)
            copies.append(
                go(
                    remote(
                        ag_send.at[side, lax.div(to, RING // 2)],
                        ag_recv.at[side, y],
                        f_ss.at[side, 2, d],
                        f_rs.at[side, 2, d],
                        y_peer(d),
                    )
                )
            )
        ag_recv[side, pl.ds(y, 1)] = ag_send[side, pl.ds(lax.div(y, RING // 2), 1)]
        return copies

    def gathered(side, h):
        return ag_recv[side, :, h].reshape(D, D)

    def kv_hop(j, c):
        src = (k_in, v_in)[c] if j == 1 else kv.at[j - 2, c]
        return go(remote(src, kv.at[j - 1, c], kv_ss.at[j - 1, c], kv_rs.at[j - 1, c], s_peer(1)))

    def q_hop(j):
        src = q_in if j == 1 else qs.at[j - 2]
        return go(remote(src, qs.at[j - 1], q_ss.at[j - 1], q_rs.at[j - 1], s_peer(-1)))

    def w_hop(j):
        src = w_own if j == 1 else ws.at[j - 2]
        return go(remote(src, ws.at[j - 1], w_ss.at[j - 1], w_rs.at[j - 1], s_peer(-1)))

    def d_hop(j, h):
        src = dm.at[h] if j == 1 else ds.at[j - 2, h]
        return go(
            remote(src, ds.at[j - 1, h], d_ss.at[j - 1, h], d_rs.at[j - 1, h], s_peer(-1))
        )

    scattered = scatter_start(0)
    kv_now = [kv_hop(1, K), kv_hop(1, V)]
    q_now = q_hop(1)

    index_row = index[...]
    for h in range(HEADS):
        rows = []
        for j in range(LEVELS):
            picked = index_row[j : j + 1]
            row = jnp.zeros((1, T), F32)
            for k in range(ROWS):
                row = jnp.where(picked == k, table[j, h, k], row)
            rows.append(row)
        rows.append(jnp.zeros((8 - LEVELS, T), F32))
        w_own[8 * h : 8 * h + 8] = jnp.concatenate(rows, axis=0)
    w_now = w_hop(1)
    spread = []
    for h in range(HEADS):
        for j in range(LEVELS):
            spread.append((iota((16, D), 0) == 8 * h + j).astype(F32))
    w_wide[...] = tn(w_own[...], jnp.concatenate(spread, axis=1), HIGH)

    def weight(h, j):
        at = (h * LEVELS + j) * D
        return w_wide[:, at : at + D]

    def window_scale(h, lanes):
        return lax.rsqrt(jnp.full((1, lanes), D * window[h], jnp.int32).astype(F32))

    token = iota((T, T), 0)
    key = iota((T, T), 1)
    pair_gap = token - key
    token_block = token >> 6
    key_block = key >> 6
    causal = pair_gap >= 0
    same_leaf = token_block == key_block
    same_pair = (token_block >> 1) == (key_block >> 1)

    def twice(half):
        return jnp.concatenate([half, half], axis=1)

    loads[2].wait()
    loads[3].wait()
    for h in range(HEADS):
        raw = nt(own[Q, h], own[K, h])
        scale0 = twice(weight(h, 0) * level_scale(BLOCK))
        scale1 = twice(weight(h, 1) * level_scale(BLOCK))
        scale2 = twice(weight(h, 2) * level_scale(2 * BLOCK))
        scale = jnp.where(same_leaf, scale0, jnp.where(same_pair, scale1, scale2))
        scale = jnp.where(causal, scale + window_scale(h, T), 0.0)
        low = (raw * scale).astype(BF)
        p_raw[h] = raw
        a_mix[h] = scale
        p_low[h] = low
        mix[h] = nn(low, own[V, h])

    def reach_q(h, j):
        limit = jnp.where(s >= j, window[h] - T * j, -T * (REACH + 1))
        return pair_gap < limit

    def reach_k(h, j):
        limit = jnp.where(s + j < shard_count, window[h] - T * j, -T * (REACH + 1))
        return -pair_gap < limit

    def far_probs(j):
        for h in range(HEADS):
            score = nt(own[K, h], qs[j - 1, h])
            p_far[j - 2, h] = jnp.where(reach_k(h, j), score, 0.0).astype(BF)

    def far_weights(j):
        spread = []
        for h in range(HEADS):
            for n in (3, 4):
                spread.append((iota((16, D), 0) == 8 * h + n).astype(F32))
        w_far[j - 1] = tn(ws[j - 1], jnp.concatenate(spread, axis=1), HIGH)

    odd = lax.rem(s, 2)
    odd_f = odd.astype(F32)
    second_f = lax.rem(lax.div(s, 2), 2).astype(F32)
    any_before = (s >= 1).astype(F32)
    any_after = (s + 1 < shard_count).astype(F32)

    def near_scale(h, wide):
        return window_scale(h, D) * any_before + wide * (odd_f * level_scale(T))

    def window_part(h, j):
        score = nt(own[Q, h], kv[j - 1, K, h])
        prob = jnp.where(reach_q(h, j), score, 0.0).astype(BF)
        return nn(prob, kv[j - 1, V, h]) * window_scale(h, D)

    q_now.wait_recv()
    q_now = q_hop(2)
    w_now.wait_recv()
    w_now = w_hop(2)
    far_weights(1)

    across, near = across_start(0, scattered)

    kv_now[K].wait_recv()
    kv_next = [kv_hop(2, K)]
    kv_now[V].wait_recv()
    kv_next.append(kv_hop(2, V))
    kv_now = kv_next
    for h in range(HEADS):
        state = tn(kv[0, K, h], kv[0, V, h]).astype(BF)
        s_near[0, h] = state
        mix[h] = mix[h] + near_scale(h, weight(h, 3)) * nn(own[Q, h], state)

    q_now.wait_recv()
    q_now = q_hop(3)
    w_now.wait_recv()
    w_now = w_hop(3)
    far_weights(2)
    far_probs(2)

    gather = gather_start(0, across, near)

    kv_now[K].wait_recv()
    kv_next = [kv_hop(3, K)]
    kv_now[V].wait_recv()
    kv_next.append(kv_hop(3, V))
    kv_now = kv_next
    for h in range(HEADS):
        mix[h] = mix[h] + window_part(h, 2)

    q_now.wait_recv()
    q_now = q_hop(4)
    w_now.wait_recv()
    far_weights(3)
    far_probs(3)

    for copy in gather:
        copy.wait_recv()
    for h in range(HEADS):
        mix[h] = mix[h] + weight(h, 5) * nn(own[Q, h], gathered(0, h))

    kv_now[K].wait_recv()
    kv_next = [kv_hop(4, K)]
    kv_now[V].wait_recv()
    kv_next.append(kv_hop(4, V))
    kv_now = kv_next
    for h in range(HEADS):
        state = tn(kv[odd, K, h], kv[odd, V, h]) + tn(kv[odd + 1, K, h], kv[odd + 1, V, h])
        state = (state * (second_f * level_scale(2 * T))).astype(BF)
        s_near[1, h] = state
        mix[h] = mix[h] + window_part(h, 3) + weight(h, 4) * nn(own[Q, h], state)

    q_now.wait_recv()
    far_probs(4)

    kv_now[K].wait_recv()
    kv_now[V].wait_recv()
    square = jnp.zeros((T, D), F32)
    cross = jnp.zeros((T, D), F32)
    for h in range(HEADS):
        mixed = mix[h] + window_part(h, 4)
        mix[h] = mixed
        square = square + mixed * mixed
        cross = cross + own[G, h].astype(F32) * gain[h : h + 1] * mixed

    both = jnp.concatenate([square, cross], axis=1)
    pick = (iota((8, 2 * D), 0) == (iota((8, 2 * D), 1) >> 7)).astype(F32)
    n_send[...] = nt(pick, both, HIGH)
    norms = []
    for d in range(1, nh):
        norms.append(go(remote(n_send, n_recv.at[hd], n_ss.at[d], n_rs.at[d], h_peer(d))))
    n_recv[pl.ds(hd, 1)] = n_send[...][None]
    for copy in norms:
        copy.wait_recv()
    sums = functools.reduce(jnp.add, [n_recv[n] for n in range(nh)])
    inv_row = lax.rsqrt(sums[0:1] * (1.0 / (HEADS * nh * D)) + EPS)
    back_row = inv_row * inv_row * inv_row * sums[1:2] * (1.0 / (HEADS * nh * D))
    both_rows = jnp.concatenate([inv_row, back_row, jnp.zeros((6, T), F32)], axis=0)
    wide = tn(both_rows, pick, HIGH)
    inv_rms = wide[:, :D]
    back = wide[:, D:]

    d_now = []
    grads = []
    for h in range(HEADS):
        given = own[G, h].astype(F32)
        grad = given * gain[h : h + 1] * inv_rms - mix[h] * back
        dm[h] = grad.astype(BF)
        grads.append(grad)
        d_now.append(d_hop(1, h))
    for h in range(HEADS):
        up = (weight(h, 5) * grads[h]).astype(BF)
        state = tn(own[Q, h], up)
        rs_send[1, :, h] = state.astype(BF).reshape(RING, PIECE, D)
    scattered = scatter_start(1)

    gain_rows = []
    for h in range(HEADS):
        scaled = mix[h] * inv_rms
        out[h] = (scaled * gain[h : h + 1]).astype(BF)
        gain_rows.append(jnp.sum(own[G, h].astype(F32) * scaled, axis=0, keepdims=True))

    lane_block = iota((8, T), 1) >> 6
    row_no = iota((8, T), 0)
    hot = jnp.concatenate(
        [(index_row[j : j + 1] == iota((ROWS, T), 0)).astype(F32) for j in range(LEVELS)], axis=0
    )
    dq = []
    dk = []
    dv = []
    for h in range(HEADS):
        grad = grads[h]
        low = dm[h]
        prob_grad = nt(low, own[V, h])
        product = jnp.where(causal, p_raw[h] * prob_grad, 0.0)
        score_grad = (prob_grad * a_mix[h]).astype(BF)
        dk.append(tn(score_grad, own[Q, h]))
        dv.append(tn(p_low[h], low))
        up1 = (near_scale(h, weight(h, 3)) * grad).astype(BF)
        up4 = (weight(h, 4) * grad).astype(BF)
        up5 = (weight(h, 5) * grad).astype(BF)
        dq.append(
            nn(score_grad, own[K, h])
            + nt(up1, s_near[0, h])
            + nt(up4, s_near[1, h])
            + nt(up5, gathered(0, h))
        )
        by_block = nt((row_no == lane_block).astype(F32), product, HIGH)
        row0 = jnp.sum(jnp.where(row_no == lane_block, by_block, 0.0), axis=0, keepdims=True)
        row1 = jnp.sum(
            jnp.where((row_no == lane_block - 1) & ((lane_block & 1) == 1), by_block, 0.0),
            axis=0,
            keepdims=True,
        )
        row2 = jnp.sum(
            jnp.where((row_no < 2) & (lane_block >= 2), by_block, 0.0), axis=0, keepdims=True
        )
        areas = jnp.concatenate(
            [
                grad * nn(own[Q, h], s_near[0, h]) * (odd_f * level_scale(T)),
                grad * nn(own[Q, h], s_near[1, h]),
                grad * nn(own[Q, h], gathered(0, h)),
            ],
            axis=1,
        )
        pick3 = (iota((8, 3 * D), 0) == (iota((8, 3 * D), 1) >> 7)).astype(F32)
        far_rows = nt(pick3, areas, HIGH)
        weight_rows = jnp.concatenate(
            [
                row0 * level_scale(BLOCK),
                row1 * level_scale(BLOCK),
                row2 * level_scale(2 * BLOCK),
                far_rows[0:3],
                jnp.zeros((2, T), F32),
            ],
            axis=0,
        )
        by_level = nt(weight_rows, hot, HIGH)
        part = jnp.zeros((8, ROWS), F32)
        for j in range(LEVELS):
            slab = by_level[:, ROWS * j : ROWS * (j + 1)]
            part = part + jnp.where(iota((8, ROWS), 0) == j, slab, 0.0)
        r_send[0, 8 * h : 8 * h + 8] = jnp.concatenate(
            [part, jnp.zeros((8, D - ROWS), F32)], axis=1
        )

    r_send[0, 16:24] = jnp.concatenate(gain_rows + [jnp.zeros((6, D), F32)], axis=0)

    def reduce_start(step):
        count, me, peer = ((ny, y, y_peer), (nz, z, z_peer))[step]
        copies = []
        for d in range(1, count):
            copies.append(
                go(
                    remote(
                        r_send.at[step],
                        r_recv.at[step, me],
                        r_ss.at[step, d],
                        r_rs.at[step, d],
                        peer(d),
                    )
                )
            )
        r_recv[step, pl.ds(me, 1)] = r_send[step][None]
        return copies

    def reduce_end(step, copies):
        for copy in copies:
            copy.wait_recv()
        count = (ny, nz)[step]
        return functools.reduce(jnp.add, [r_recv[step, n] for n in range(count)])

    reduced = reduce_start(0)

    def d_step(j, forward):
        later = []
        for h in range(HEADS):
            d_now[h].wait_recv()
            if forward:
                later.append(d_hop(j + 1, h))
        return later

    def from_far(j):
        for h in range(HEADS):
            scale = window_scale(h, D)
            grad = ds[j - 1, h]
            dv[h] = dv[h] + nn(p_far[j - 2, h], grad) * scale
            back_score = jnp.where(reach_k(h, j), nt(own[V, h], grad), 0.0).astype(BF)
            dk[h] = dk[h] + nn(back_score, qs[j - 1, h]) * scale

    def to_far(j):
        for h in range(HEADS):
            back_score = jnp.where(reach_q(h, j), nt(dm[h], kv[j - 1, V, h]), 0.0).astype(BF)
            dq[h] = dq[h] + nn(back_score, kv[j - 1, K, h]) * window_scale(h, D)

    def far_weight(j, h, n):
        at = (2 * h + n) * D
        return w_far[j - 1, :, at : at + D]

    d_now = d_step(1, True)
    across, near = across_start(1, scattered)
    even_f = 1.0 - odd_f
    states = []
    for h in range(HEADS):
        scale = window_scale(h, D) * any_after + far_weight(1, h, 0) * (even_f * level_scale(T))
        states.append(tn(qs[0, h], (scale * ds[0, h].astype(F32)).astype(BF)))
    to_far(2)

    d_now = d_step(2, True)
    to_far(3)
    gather = gather_start(1, across, near)
    from_far(2)

    d_now = d_step(3, True)
    reduced = reduce_end(0, reduced)
    r_send[1] = reduced
    reduced = reduce_start(1)
    to_far(4)
    for h in range(HEADS):
        dq_out[h] = dq[h].astype(BF)
    from_far(3)
    first_f = 1.0 - second_f
    for h in range(HEADS):
        for n in range(2):
            slot = 1 - odd + n
            at = (2 * h + 1) * D
            scale = w_far[slot, :, at : at + D] * (first_f * level_scale(2 * T))
            states[h] = states[h] + tn(
                qs[slot, h], (scale * ds[slot, h].astype(F32)).astype(BF)
            )

    for copy in gather:
        copy.wait_recv()
    d_step(4, False)
    from_far(4)
    for h in range(HEADS):
        state = (states[h] + gathered(1, h).astype(F32)).astype(BF)
        dk_out[h] = (dk[h] + nt(own[V, h], state)).astype(BF)
        dv_out[h] = (dv[h] + nn(own[K, h], state)).astype(BF)

    total = reduce_end(1, reduced)
    for h in range(HEADS):
        table_out[:, h] = total[8 * h : 8 * h + LEVELS, 0:ROWS]
    gain_out[...] = total[16 : 16 + HEADS]
    for copy in sent:
        copy.wait_send()


def shards(
    dims,
    query_rows,
    key_rows,
    value_rows,
    norm_gain,
    level_table,
    level_index,
    window_length,
    out_grad,
):
    big = jax.ShapeDtypeStruct((HEADS, T, D), BF)
    nz, ny, nh = dims
    vmem = pl.BlockSpec(memory_space=pltpu.VMEM)
    smem = pl.BlockSpec(memory_space=pltpu.SMEM)
    far = pl.BlockSpec(memory_space=pl.ANY)
    dma = pltpu.SemaphoreType.DMA
    layer, dq, dk, dv, table_grad, gain_grad = pl.pallas_call(
        functools.partial(kernel, dims),
        out_shape=(
            big,
            big,
            big,
            big,
            jax.ShapeDtypeStruct((LEVELS, HEADS, ROWS), F32),
            jax.ShapeDtypeStruct((HEADS, D), F32),
        ),
        in_specs=[far, far, far, far, vmem, smem, vmem, smem],
        out_specs=[vmem] * 6,
        scratch_shapes=[
            pltpu.VMEM((4, HEADS, T, D), BF),
            pltpu.VMEM((REACH, 2, HEADS, T, D), BF),
            pltpu.VMEM((REACH, HEADS, T, D), BF),
            pltpu.VMEM((REACH, HEADS, T, D), BF),
            pltpu.VMEM((3, 16, T), F32),
            pltpu.VMEM((16, T), F32),
            pltpu.VMEM((T, HEADS * LEVELS * D), F32),
            pltpu.VMEM((3, T, HEADS * 2 * D), F32),
            pltpu.VMEM((HEADS, T, T), F32),
            pltpu.VMEM((HEADS, T, T), F32),
            pltpu.VMEM((HEADS, T, T), BF),
            pltpu.VMEM((3, HEADS, T, T), BF),
            pltpu.VMEM((2, HEADS, D, D), BF),
            pltpu.VMEM((HEADS, T, D), F32),
            pltpu.VMEM((HEADS, T, D), BF),
            pltpu.VMEM((2, RING, HEADS, PIECE, D), BF),
            pltpu.VMEM((2, RING, HEADS, PIECE, D), BF),
            pltpu.VMEM((2, HEADS, PIECE, D), BF),
            pltpu.VMEM((2, nz, HEADS, PIECE, D), BF),
            pltpu.VMEM((2, 2, HEADS, PIECE, D), BF),
            pltpu.VMEM((2, RING, HEADS, PIECE, D), BF),
            pltpu.VMEM((8, T), F32),
            pltpu.VMEM((nh, 8, T), F32),
            pltpu.VMEM((2, 24, D), F32),
            pltpu.VMEM((2, RING, 24, D), F32),
            dma((4,)),
            dma((REACH, 2)),
            dma((REACH, 2)),
            dma((REACH,)),
            dma((REACH,)),
            dma((REACH, HEADS)),
            dma((REACH, HEADS)),
            dma((3,)),
            dma((3,)),
            dma((2, 3, RING)),
            dma((2, 3, RING)),
            dma((RING,)),
            dma((RING,)),
            dma((2, RING)),
            dma((2, RING)),
        ],
        compiler_params=pltpu.CompilerParams(
            collective_id=0, has_side_effects=True, vmem_limit_bytes=40 * 1024 * 1024
        ),
    )(
        query_rows,
        key_rows,
        value_rows,
        out_grad,
        norm_gain,
        jnp.transpose(level_table, (2, 1, 0)),
        level_index.T,
        window_length,
    )
    return layer, dq, dk, dv, jnp.transpose(table_grad, (2, 1, 0)), gain_grad


def solution(mesh):
    heads = mesh.shape["head"]
    dims = (mesh.shape["seq"] // RING, RING, heads)
    torus = Mesh(mesh.devices.reshape(*dims), ("seq_0", "seq_1", "head"))
    seq = ("seq_0", "seq_1")
    rows = P("head", seq, None)
    return jax.shard_map(
        functools.partial(shards, dims),
        mesh=torus,
        in_specs=(
            rows,
            rows,
            rows,
            P("head", None),
            P(None, "head", None),
            P(seq, None),
            P("head"),
            rows,
        ),
        out_specs=(rows, rows, rows, rows, P(None, "head", None), P("head", None)),
        check_vma=False,
    )
```

```python
import functools
import math

import jax
import jax.numpy as jnp
from jax import lax
from jax.experimental import pallas as pl
from jax.experimental.pallas import tpu as pltpu
from jax.sharding import Mesh
from jax.sharding import PartitionSpec as P

BLOCK = 64
LEVELS = 6
ROWS = 16
REACH = 4
HEADS = 2
T = 256
D = 128
RING = 8
PIECE = D // RING
EPS = 1e-06
BF = jnp.bfloat16
F32 = jnp.float32
HIGH = lax.Precision.HIGHEST
MESH = pl.DeviceIdType.MESH


def level_scale(group_len):
    return 1.0 / math.sqrt(group_len * D)


def nn(a, b):
    return lax.dot_general(a, b, (((1,), (0,)), ((), ())), preferred_element_type=F32)


def nt(a, b, precision=None):
    return lax.dot_general(
        a, b, (((1,), (1,)), ((), ())), precision=precision, preferred_element_type=F32
    )


def tn(a, b, precision=None):
    return lax.dot_general(
        a, b, (((0,), (0,)), ((), ())), precision=precision, preferred_element_type=F32
    )


def iota(shape, dim):
    return lax.broadcasted_iota(jnp.int32, shape, dim)


def kernel(
    dims,
    q_in,
    k_in,
    v_in,
    g_in,
    gain_in,
    table_in,
    index_in,
    window_in,
    out_to,
    dq_to,
    dk_to,
    dv_to,
    table_to,
    gain_to,
    out,
    dq_out,
    dk_out,
    dv_out,
    table_out,
    gain_out,
    gain,
    table,
    index,
    window,
    own,
    kv,
    qs,
    ds,
    ws,
    w_own,
    w_wide,
    w_far,
    p_raw,
    a_mix,
    p_low,
    p_far,
    s_near,
    mix,
    dm,
    rs_send,
    rs_recv,
    z_send,
    z_recv,
    ag_send,
    ag_recv,
    n_send,
    n_recv,
    r_send,
    r_recv,
    in_sem,
    out_sem,
    kv_ss,
    kv_rs,
    q_ss,
    q_rs,
    d_ss,
    d_rs,
    w_ss,
    w_rs,
    f_ss,
    f_rs,
    n_ss,
    n_rs,
    r_ss,
    r_rs,
    below,
    above,
):
    nz, ny, nh = dims
    z = lax.axis_index("seq_0")
    y = lax.axis_index("seq_1")
    hd = lax.axis_index("head")
    s = z * ny + y
    shard_count = nz * ny

    def y_peer(d):
        return (z, lax.rem(y + d, ny), hd)

    def z_peer(d):
        return (lax.rem(z + d + nz, nz), y, hd)

    def h_peer(d):
        return (z, y, lax.rem(hd + d, nh))

    def s_peer(d):
        to = lax.rem(s + d + shard_count, shard_count)
        return (lax.div(to, ny), lax.rem(to, ny), hd)

    def remote(src, dst, ss, rs, to):
        return pltpu.make_async_remote_copy(
            src_ref=src, dst_ref=dst, send_sem=ss, recv_sem=rs, device_id=to, device_id_type=MESH
        )

    sent = []

    def on(condition, action):
        if condition is None:
            action()
        else:
            pl.when(condition)(action)

    def go(copy, condition=None):
        on(condition, copy.start)
        sent.append((copy, condition))
        return copy

    results = (
        (out, out_to),
        (dq_out, dq_to),
        (dk_out, dk_to),
        (dv_out, dv_to),
        (table_out, table_to),
        (gain_out, gain_to),
    )
    stores = []

    def store(n):
        stores.append(pltpu.make_async_copy(*results[n], out_sem.at[n]))
        stores[-1].start()

    barrier = pltpu.get_barrier_semaphore()
    last = shard_count - 1
    peers = [(s_peer(1), s < last), (s_peer(-1), s > 0)]
    if nz > 1:
        peers += [(z_peer(1), z < nz - 1), (z_peer(-1), z > 0)]
    peers += [(y_peer(d), None) for d in range(1, ny)]
    peers += [(h_peer(d), None) for d in range(1, nh)]

    def signal(sem, peer):
        pl.semaphore_signal(sem, inc=1, device_id=peer, device_id_type=MESH)

    expected = 0
    for peer, condition in peers:
        on(condition, functools.partial(signal, barrier, peer))
        expected = expected + (1 if condition is None else condition.astype(jnp.int32))

    loads = []
    targets = (own.at[0], own.at[1], own.at[2], own.at[3], table, index, window, gain)
    arrays = (k_in, v_in, q_in, g_in, table_in, index_in, window_in, gain_in)
    for n, (ref, target) in enumerate(zip(arrays, targets)):
        load = pltpu.make_async_copy(ref, target, in_sem.at[n])
        load.start()
        loads.append(load)
    loads[0].wait()
    loads[1].wait()
    K, V, Q, G = 0, 1, 2, 3

    for h in range(HEADS):
        state = tn(own[K, h], own[V, h])
        rs_send[0, :, h] = state.astype(BF).reshape(RING, PIECE, D)

    for j in range(1, REACH + 1):

        def clear_before(j=j):
            kv[j - 1] = jnp.zeros((2, HEADS, T, D), BF)

        def clear_after(j=j):
            qs[j - 1] = jnp.zeros((HEADS, T, D), BF)
            ds[j - 1] = jnp.zeros((HEADS, T, D), BF)
            if j < REACH:
                ws[j - 1] = jnp.zeros((16, T), F32)

        pl.when(s < j)(clear_before)
        pl.when(s + j > last)(clear_after)

    pl.semaphore_wait(barrier, expected)

    def scatter_start(side):
        copies = []
        for d in range(1, ny):
            to = lax.rem(y + d, ny)
            copies.append(
                go(
                    remote(
                        rs_send.at[side, to],
                        rs_recv.at[side, y],
                        f_ss.at[side, 0, d],
                        f_rs.at[side, 0, d],
                        y_peer(d),
                    )
                )
            )
        rs_recv[side, pl.ds(y, 1)] = rs_send[side, pl.ds(y, 1)]
        return copies

    def comes(side, d):
        return z >= d if side == 0 else z + d < nz

    def leaves(side, d):
        return z + d < nz if side == 0 else z >= d

    def across_start(side, scattered):
        for copy in scattered:
            copy.wait_recv()
        half = RING // 2
        pieces = [rs_recv[side, n].astype(F32) for n in range(RING)]
        low = functools.reduce(jnp.add, pieces[:half])
        upper = functools.reduce(jnp.add, pieces[half:])
        z_send[side] = (low + upper).astype(BF)
        copies = []
        for d in range(1, nz):
            copies.append(
                go(
                    remote(
                        z_send.at[side],
                        z_recv.at[side, d],
                        f_ss.at[side, 1, d],
                        f_rs.at[side, 1, d],
                        z_peer(d if side == 0 else -d),
                    ),
                    leaves(side, d),
                )
            )
        return copies, (low if side == 0 else upper)

    def gather_start(side, across, near):
        total = jnp.zeros((HEADS, PIECE, D), F32)
        for d in range(1, nz):
            counts = comes(side, d)
            on(counts, across[d - 1].wait_recv)
            other = lax.rem((z - d if side == 0 else z + d) + nz, nz)
            scale = jnp.where(
                lax.div(other, 2) == lax.div(z, 2),
                level_scale(T * 8),
                jnp.where(
                    lax.div(other, 4) == lax.div(z, 4), level_scale(T * 16), level_scale(T * 32)
                ),
            )
            total = total + jnp.where(counts, z_recv[side, d].astype(F32) * scale, 0.0)
        with_near = (total + near * level_scale(T * 4)).astype(BF)
        plain = total.astype(BF)
        ag_send[side, 0] = plain if side == 0 else with_near
        ag_send[side, 1] = with_near if side == 0 else plain
        copies = []
        for d in range(1, ny):
            to = lax.rem(y + d, ny)
            copies.append(
                go(
                    remote(
                        ag_send.at[side, lax.div(to, RING // 2)],
                        ag_recv.at[side, y],
                        f_ss.at[side, 2, d],
                        f_rs.at[side, 2, d],
                        y_peer(d),
                    )
                )
            )
        ag_recv[side, pl.ds(y, 1)] = ag_send[side, pl.ds(lax.div(y, RING // 2), 1)]
        return copies

    def gathered(side, h):
        return ag_recv[side, :, h].reshape(D, D)

    def before(j):
        return s >= j

    def after(j):
        return s + j <= last

    def forward(src, dst, ss, rs, j):
        return go(remote(src, dst, ss, rs, s_peer(1)), (s >= j - 1) & (s < last))

    def backward(src, dst, ss, rs, j):
        return go(remote(src, dst, ss, rs, s_peer(-1)), (s + j - 1 <= last) & (s > 0))

    def kv_hop(j, c):
        src = (k_in, v_in)[c] if j == 1 else kv.at[j - 2, c]
        return forward(src, kv.at[j - 1, c], kv_ss.at[j - 1, c], kv_rs.at[j - 1, c], j)

    def q_hop(j):
        src = q_in if j == 1 else qs.at[j - 2]
        return backward(src, qs.at[j - 1], q_ss.at[j - 1], q_rs.at[j - 1], j)

    def w_hop(j):
        src = w_own if j == 1 else ws.at[j - 2]
        return backward(src, ws.at[j - 1], w_ss.at[j - 1], w_rs.at[j - 1], j)

    def d_hop(j, h):
        src = dm.at[h] if j == 1 else ds.at[j - 2, h]
        return backward(src, ds.at[j - 1, h], d_ss.at[j - 1, h], d_rs.at[j - 1, h], j)

    def kv_step(j, c):
        on(before(j), kv_now[c].wait_recv)
        if j < REACH:
            kv_now[c] = kv_hop(j + 1, c)

    def q_step(j):
        on(after(j), q_now[0].wait_recv)
        if j < REACH:
            q_now[0] = q_hop(j + 1)
            on(after(j), w_now[0].wait_recv)
        if j < REACH - 1:
            w_now[0] = w_hop(j + 1)

    scattered = scatter_start(0)
    kv_now = [kv_hop(1, K), kv_hop(1, V)]
    q_now = [q_hop(1)]

    for load in loads[2:]:
        load.wait()
    index_row = index[...]
    for h in range(HEADS):
        rows = []
        for j in range(LEVELS):
            picked = index_row[j : j + 1]
            row = jnp.zeros((1, T), F32)
            for k in range(ROWS):
                row = jnp.where(picked == k, table[j, h, k], row)
            rows.append(row)
        rows.append(jnp.zeros((8 - LEVELS, T), F32))
        w_own[8 * h : 8 * h + 8] = jnp.concatenate(rows, axis=0)
    w_now = [w_hop(1)]
    spread = []
    for h in range(HEADS):
        for j in range(LEVELS):
            spread.append((iota((16, D), 0) == 8 * h + j).astype(F32))
    w_wide[...] = tn(w_own[...], jnp.concatenate(spread, axis=1), HIGH)

    def weight(h, j):
        at = (h * LEVELS + j) * D
        return w_wide[:, at : at + D]

    def window_scale(h, lanes):
        return lax.rsqrt(jnp.full((1, lanes), D * window[h], jnp.int32).astype(F32))

    token = iota((T, T), 0)
    key = iota((T, T), 1)
    pair_gap = token - key
    token_block = token >> 6
    key_block = key >> 6
    causal = pair_gap >= 0
    same_leaf = token_block == key_block
    same_pair = (token_block >> 1) == (key_block >> 1)

    def twice(half):
        return jnp.concatenate([half, half], axis=1)

    for h in range(HEADS):
        raw = nt(own[Q, h], own[K, h])
        scale0 = twice(weight(h, 0) * level_scale(BLOCK))
        scale1 = twice(weight(h, 1) * level_scale(BLOCK))
        scale2 = twice(weight(h, 2) * level_scale(2 * BLOCK))
        scale = jnp.where(same_leaf, scale0, jnp.where(same_pair, scale1, scale2))
        scale = jnp.where(causal, scale + window_scale(h, T), 0.0)
        low = (raw * scale).astype(BF)
        p_raw[h] = raw
        a_mix[h] = scale
        p_low[h] = low
        mix[h] = nn(low, own[V, h])

    def reach_q(h, j):
        limit = jnp.where(s >= j, window[h] - T * j, -T * (REACH + 1))
        return pair_gap < limit

    def reach_k(h, j):
        limit = jnp.where(s + j < shard_count, window[h] - T * j, -T * (REACH + 1))
        return -pair_gap < limit

    def far_probs(j):
        for h in range(HEADS):
            score = nt(own[K, h], qs[j - 1, h])
            p_far[j - 2, h] = jnp.where(reach_k(h, j), score, 0.0).astype(BF)

    def far_weights(j):
        spread = []
        for h in range(HEADS):
            for n in (3, 4):
                spread.append((iota((16, D), 0) == 8 * h + n).astype(F32))
        w_far[j - 1] = tn(ws[j - 1], jnp.concatenate(spread, axis=1), HIGH)

    odd = lax.rem(s, 2)
    odd_f = odd.astype(F32)
    second_f = lax.rem(lax.div(s, 2), 2).astype(F32)
    any_before = (s >= 1).astype(F32)
    any_after = (s + 1 < shard_count).astype(F32)

    def near_scale(h, wide):
        return window_scale(h, D) * any_before + wide * (odd_f * level_scale(T))

    def window_prob(h, j):
        score = nt(own[Q, h], kv[j - 1, K, h])
        return jnp.where(reach_q(h, j), score, 0.0).astype(BF)

    def window_part(h, j):
        return nn(window_prob(h, j), kv[j - 1, V, h]) * window_scale(h, D)

    if nz > 1:
        on(z > 0, lambda: pl.semaphore_wait(below, 1))
        on(z < nz - 1, lambda: signal(below, z_peer(1)))
        for d in range(1, nz):
            on(z >= d, functools.partial(signal, above, z_peer(-d)))

    kv_step(1, K)
    q_step(1)
    kv_step(1, V)
    if nz > 1:
        on(z < nz - 1, lambda: pl.semaphore_wait(above, nz - 1 - z))
    across, near = across_start(0, scattered)
    for h in range(HEADS):
        state = tn(kv[0, K, h], kv[0, V, h]).astype(BF)
        s_near[0, h] = state
        mix[h] = mix[h] + near_scale(h, weight(h, 3)) * nn(own[Q, h], state)

    kv_step(2, K)
    q_step(2)
    far_weights(1)
    kv_step(2, V)
    gather = gather_start(0, across, near)
    for h in range(HEADS):
        mix[h] = mix[h] + window_part(h, 2)

    kv_step(3, K)
    q_step(3)
    far_weights(2)
    far_probs(2)
    kv_step(3, V)
    for h in range(HEADS):
        state = tn(kv[odd, K, h], kv[odd, V, h]) + tn(kv[odd + 1, K, h], kv[odd + 1, V, h])
        state = (state * (second_f * level_scale(2 * T))).astype(BF)
        s_near[1, h] = state
        mix[h] = mix[h] + window_part(h, 3) + weight(h, 4) * nn(own[Q, h], state)
    for copy in gather:
        copy.wait_recv()
    for h in range(HEADS):
        mix[h] = mix[h] + weight(h, 5) * nn(own[Q, h], gathered(0, h))

    kv_step(4, K)
    last_probs = [window_prob(h, 4) for h in range(HEADS)]
    kv_step(4, V)
    square = jnp.zeros((T, D), F32)
    cross = jnp.zeros((T, D), F32)
    for h in range(HEADS):
        mixed = mix[h] + nn(last_probs[h], kv[3, V, h]) * window_scale(h, D)
        mix[h] = mixed
        square = square + mixed * mixed
        cross = cross + own[G, h].astype(F32) * gain[h : h + 1] * mixed

    both = jnp.concatenate([square, cross], axis=1)
    pick = (iota((8, 2 * D), 0) == (iota((8, 2 * D), 1) >> 7)).astype(F32)
    n_send[...] = nt(pick, both, HIGH)
    norms = []
    for d in range(1, nh):
        norms.append(go(remote(n_send, n_recv.at[hd], n_ss.at[d], n_rs.at[d], h_peer(d))))
    n_recv[pl.ds(hd, 1)] = n_send[...][None]
    for copy in norms:
        copy.wait_recv()
    sums = functools.reduce(jnp.add, [n_recv[n] for n in range(nh)])
    inv_row = lax.rsqrt(sums[0:1] * (1.0 / (HEADS * nh * D)) + EPS)
    back_row = inv_row * inv_row * inv_row * sums[1:2] * (1.0 / (HEADS * nh * D))
    both_rows = jnp.concatenate([inv_row, back_row, jnp.zeros((6, T), F32)], axis=0)
    wide = tn(both_rows, pick, HIGH)
    inv_rms = wide[:, :D]
    back = wide[:, D:]

    grads = []
    for h in range(HEADS):
        given = own[G, h].astype(F32)
        grad = given * gain[h : h + 1] * inv_rms - mix[h] * back
        dm[h] = grad.astype(BF)
        grads.append(grad)
    for h in range(HEADS):
        up = (weight(h, 5) * grads[h]).astype(BF)
        state = tn(own[Q, h], up)
        rs_send[1, :, h] = state.astype(BF).reshape(RING, PIECE, D)
    scattered = scatter_start(1)
    d_now = [d_hop(1, h) for h in range(HEADS)]

    gain_rows = []
    for h in range(HEADS):
        scaled = mix[h] * inv_rms
        out[h] = (scaled * gain[h : h + 1]).astype(BF)
        gain_rows.append(jnp.sum(own[G, h].astype(F32) * scaled, axis=0, keepdims=True))

    store(0)

    lane_block = iota((8, T), 1) >> 6
    row_no = iota((8, T), 0)
    hot = jnp.concatenate(
        [(index_row[j : j + 1] == iota((ROWS, T), 0)).astype(F32) for j in range(LEVELS)], axis=0
    )
    dq = []
    dk = []
    dv = []
    for h in range(HEADS):
        grad = grads[h]
        low = dm[h]
        prob_grad = nt(low, own[V, h])
        product = jnp.where(causal, p_raw[h] * prob_grad, 0.0)
        score_grad = (prob_grad * a_mix[h]).astype(BF)
        dk.append(tn(score_grad, own[Q, h]))
        dv.append(tn(p_low[h], low))
        up1 = (near_scale(h, weight(h, 3)) * grad).astype(BF)
        up4 = (weight(h, 4) * grad).astype(BF)
        up5 = (weight(h, 5) * grad).astype(BF)
        dq.append(
            nn(score_grad, own[K, h])
            + nt(up1, s_near[0, h])
            + nt(up4, s_near[1, h])
            + nt(up5, gathered(0, h))
        )
        by_block = nt((row_no == lane_block).astype(F32), product, HIGH)
        row0 = jnp.sum(jnp.where(row_no == lane_block, by_block, 0.0), axis=0, keepdims=True)
        row1 = jnp.sum(
            jnp.where((row_no == lane_block - 1) & ((lane_block & 1) == 1), by_block, 0.0),
            axis=0,
            keepdims=True,
        )
        row2 = jnp.sum(
            jnp.where((row_no < 2) & (lane_block >= 2), by_block, 0.0), axis=0, keepdims=True
        )
        areas = jnp.concatenate(
            [
                grad * nn(own[Q, h], s_near[0, h]) * (odd_f * level_scale(T)),
                grad * nn(own[Q, h], s_near[1, h]),
                grad * nn(own[Q, h], gathered(0, h)),
            ],
            axis=1,
        )
        pick3 = (iota((8, 3 * D), 0) == (iota((8, 3 * D), 1) >> 7)).astype(F32)
        far_rows = nt(pick3, areas, HIGH)
        weight_rows = jnp.concatenate(
            [
                row0 * level_scale(BLOCK),
                row1 * level_scale(BLOCK),
                row2 * level_scale(2 * BLOCK),
                far_rows[0:3],
                jnp.zeros((2, T), F32),
            ],
            axis=0,
        )
        by_level = nt(weight_rows, hot, HIGH)
        part = jnp.zeros((8, ROWS), F32)
        for j in range(LEVELS):
            slab = by_level[:, ROWS * j : ROWS * (j + 1)]
            part = part + jnp.where(iota((8, ROWS), 0) == j, slab, 0.0)
        r_send[0, 8 * h : 8 * h + 8] = jnp.concatenate(
            [part, jnp.zeros((8, D - ROWS), F32)], axis=1
        )

    r_send[0, 16:24] = jnp.concatenate(gain_rows + [jnp.zeros((6, D), F32)], axis=0)

    def reduce_start(step):
        count, me, peer = ((ny, y, y_peer), (nz, z, z_peer))[step]
        copies = []
        for d in range(1, count):
            copies.append(
                go(
                    remote(
                        r_send.at[step],
                        r_recv.at[step, me],
                        r_ss.at[step, d],
                        r_rs.at[step, d],
                        peer(d),
                    )
                )
            )
        r_recv[step, pl.ds(me, 1)] = r_send[step][None]
        return copies

    def reduce_end(step, copies):
        for copy in copies:
            copy.wait_recv()
        count = (ny, nz)[step]
        return functools.reduce(jnp.add, [r_recv[step, n] for n in range(count)])

    reduced = reduce_start(0)

    def d_step(j):
        for h in range(HEADS):
            on(after(j), d_now[h].wait_recv)
            if j < REACH:
                d_now[h] = d_hop(j + 1, h)

    def from_far(j):
        for h in range(HEADS):
            scale = window_scale(h, D)
            grad = ds[j - 1, h]
            dv[h] = dv[h] + nn(p_far[j - 2, h], grad) * scale
            back_score = jnp.where(reach_k(h, j), nt(own[V, h], grad), 0.0).astype(BF)
            dk[h] = dk[h] + nn(back_score, qs[j - 1, h]) * scale

    def to_far(j):
        for h in range(HEADS):
            back_score = jnp.where(reach_q(h, j), nt(dm[h], kv[j - 1, V, h]), 0.0).astype(BF)
            dq[h] = dq[h] + nn(back_score, kv[j - 1, K, h]) * window_scale(h, D)

    def far_weight(j, h, n):
        at = (2 * h + n) * D
        return w_far[j - 1, :, at : at + D]

    d_step(1)
    across, near = across_start(1, scattered)
    far_weights(3)
    far_probs(3)
    even_f = 1.0 - odd_f
    states = []
    for h in range(HEADS):
        scale = window_scale(h, D) * any_after + far_weight(1, h, 0) * (even_f * level_scale(T))
        states.append(tn(qs[0, h], (scale * ds[0, h].astype(F32)).astype(BF)))
    to_far(2)

    d_step(2)
    r_send[1] = reduce_end(0, reduced)
    reduced = reduce_start(1)
    to_far(3)
    from_far(2)

    d_step(3)
    q_step(4)
    far_probs(4)
    to_far(4)
    for h in range(HEADS):
        dq_out[h] = dq[h].astype(BF)
    store(1)
    from_far(3)
    first_f = 1.0 - second_f
    for h in range(HEADS):
        for n in range(2):
            slot = 1 - odd + n
            at = (2 * h + 1) * D
            scale = w_far[slot, :, at : at + D] * (first_f * level_scale(2 * T))
            states[h] = states[h] + tn(
                qs[slot, h], (scale * ds[slot, h].astype(F32)).astype(BF)
            )

    d_step(4)
    from_far(4)
    gather = gather_start(1, across, near)
    for copy in gather:
        copy.wait_recv()
    for h in range(HEADS):
        state = (states[h] + gathered(1, h).astype(F32)).astype(BF)
        dk_out[h] = (dk[h] + nt(own[V, h], state)).astype(BF)
        dv_out[h] = (dv[h] + nn(own[K, h], state)).astype(BF)

    store(2)
    store(3)
    total = reduce_end(1, reduced)
    for h in range(HEADS):
        table_out[:, h] = total[8 * h : 8 * h + LEVELS, 0:ROWS]
    gain_out[...] = total[16 : 16 + HEADS]
    store(4)
    store(5)
    for copy, condition in sent:
        on(condition, copy.wait_send)
    for copy in stores:
        copy.wait()


def place_kernel(*refs):
    for n in range(6):
        refs[6 + n][...] = refs[n][...]


def shards(
    dims,
    query_rows,
    key_rows,
    value_rows,
    norm_gain,
    level_table,
    level_index,
    window_length,
    out_grad,
):
    big = jax.ShapeDtypeStruct((HEADS, T, D), BF)
    nz, ny, nh = dims
    far = pl.BlockSpec(memory_space=pl.ANY)
    vmem = pl.BlockSpec(memory_space=pltpu.VMEM)
    dma = pltpu.SemaphoreType.DMA
    results = pl.pallas_call(
        functools.partial(kernel, dims),
        out_shape=(
            big,
            big,
            big,
            big,
            jax.ShapeDtypeStruct((LEVELS, HEADS, ROWS), F32),
            jax.ShapeDtypeStruct((HEADS, D), F32),
        ),
        in_specs=[far] * 8,
        out_specs=[far] * 6,
        scratch_shapes=[
            pltpu.VMEM((HEADS, T, D), BF),
            pltpu.VMEM((HEADS, T, D), BF),
            pltpu.VMEM((HEADS, T, D), BF),
            pltpu.VMEM((HEADS, T, D), BF),
            pltpu.VMEM((LEVELS, HEADS, ROWS), F32),
            pltpu.VMEM((HEADS, D), F32),
            pltpu.VMEM((HEADS, D), F32),
            pltpu.SMEM((LEVELS, HEADS, ROWS), F32),
            pltpu.VMEM((LEVELS, T), jnp.int32),
            pltpu.SMEM((HEADS,), jnp.int32),
            pltpu.VMEM((4, HEADS, T, D), BF),
            pltpu.VMEM((REACH, 2, HEADS, T, D), BF),
            pltpu.VMEM((REACH, HEADS, T, D), BF),
            pltpu.VMEM((REACH, HEADS, T, D), BF),
            pltpu.VMEM((3, 16, T), F32),
            pltpu.VMEM((16, T), F32),
            pltpu.VMEM((T, HEADS * LEVELS * D), F32),
            pltpu.VMEM((3, T, HEADS * 2 * D), F32),
            pltpu.VMEM((HEADS, T, T), F32),
            pltpu.VMEM((HEADS, T, T), F32),
            pltpu.VMEM((HEADS, T, T), BF),
            pltpu.VMEM((3, HEADS, T, T), BF),
            pltpu.VMEM((2, HEADS, D, D), BF),
            pltpu.VMEM((HEADS, T, D), F32),
            pltpu.VMEM((HEADS, T, D), BF),
            pltpu.VMEM((2, RING, HEADS, PIECE, D), BF),
            pltpu.VMEM((2, RING, HEADS, PIECE, D), BF),
            pltpu.VMEM((2, HEADS, PIECE, D), BF),
            pltpu.VMEM((2, nz, HEADS, PIECE, D), BF),
            pltpu.VMEM((2, 2, HEADS, PIECE, D), BF),
            pltpu.VMEM((2, RING, HEADS, PIECE, D), BF),
            pltpu.VMEM((8, T), F32),
            pltpu.VMEM((nh, 8, T), F32),
            pltpu.VMEM((2, 24, D), F32),
            pltpu.VMEM((2, RING, 24, D), F32),
            dma((8,)),
            dma((6,)),
            dma((REACH, 2)),
            dma((REACH, 2)),
            dma((REACH,)),
            dma((REACH,)),
            dma((REACH, HEADS)),
            dma((REACH, HEADS)),
            dma((3,)),
            dma((3,)),
            dma((2, 3, RING)),
            dma((2, 3, RING)),
            dma((RING,)),
            dma((RING,)),
            dma((2, RING)),
            dma((2, RING)),
            pltpu.SemaphoreType.REGULAR,
            pltpu.SemaphoreType.REGULAR,
        ],
        compiler_params=pltpu.CompilerParams(
            collective_id=0, has_side_effects=True, vmem_limit_bytes=56 * 1024 * 1024
        ),
    )(
        query_rows,
        key_rows,
        value_rows,
        out_grad,
        norm_gain,
        jnp.transpose(level_table, (2, 1, 0)),
        level_index.T,
        window_length,
    )
    layer, dq, dk, dv, table_grad, gain_grad = pl.pallas_call(
        place_kernel,
        out_shape=[jax.ShapeDtypeStruct(r.shape, r.dtype) for r in results],
        in_specs=[vmem] * 6,
        out_specs=[vmem] * 6,
    )(*results)
    return layer, dq, dk, dv, jnp.transpose(table_grad, (2, 1, 0)), gain_grad


def solution(mesh):
    heads = mesh.shape["head"]
    dims = (mesh.shape["seq"] // RING, RING, heads)
    torus = Mesh(mesh.devices.reshape(*dims), ("seq_0", "seq_1", "head"))
    seq = ("seq_0", "seq_1")
    rows = P("head", seq, None)
    return jax.shard_map(
        functools.partial(shards, dims),
        mesh=torus,
        in_specs=(
            rows,
            rows,
            rows,
            P("head", None),
            P(None, "head", None),
            P(seq, None),
            P("head"),
            rows,
        ),
        out_specs=(rows, rows, rows, rows, P(None, "head", None), P("head", None)),
        check_vma=False,
    )
```

```python
import functools
import math

import jax
import jax.numpy as jnp
from jax import lax
from jax.experimental import pallas as pl
from jax.experimental.pallas import tpu as pltpu
from jax.sharding import Mesh
from jax.sharding import PartitionSpec as P

BLOCK = 64
LEVELS = 6
ROWS = 16
REACH = 4
HEADS = 2
T = 256
D = 128
RING = 8
PIECE = D // RING
EPS = 1e-06
BF = jnp.bfloat16
F32 = jnp.float32
MESH = pl.DeviceIdType.MESH


def level_scale(group_len):
    return 1.0 / math.sqrt(group_len * D)


def nn(a, b):
    return lax.dot_general(a, b, (((1,), (0,)), ((), ())), preferred_element_type=F32)


def nt(a, b):
    return lax.dot_general(a, b, (((1,), (1,)), ((), ())), preferred_element_type=F32)


def tn(a, b):
    return lax.dot_general(a, b, (((0,), (0,)), ((), ())), preferred_element_type=F32)


def halves(x):
    high = x.astype(BF)
    return high, (x - high.astype(F32)).astype(BF)


def pick_nt(ones, x):
    high, low = halves(x)
    return nt(ones, high) + nt(ones, low)


def pick_tn(x, ones):
    high, low = halves(x)
    return tn(high, ones) + tn(low, ones)


def iota(shape, dim):
    return lax.broadcasted_iota(jnp.int32, shape, dim)


def kernel(
    dims,
    q_in,
    k_in,
    v_in,
    g_in,
    gain_in,
    table_in,
    index_in,
    window_in,
    out_to,
    dq_to,
    dk_to,
    dv_to,
    table_to,
    gain_to,
    out,
    dq_out,
    dk_out,
    dv_out,
    table_out,
    gain_out,
    gain,
    table,
    index,
    window,
    own,
    kv,
    qs,
    ds,
    ws,
    w_own,
    w_wide,
    w_far,
    p_raw,
    a_mix,
    p_low,
    p_far,
    s_near,
    mix,
    dm,
    rs_send,
    rs_recv,
    z_send,
    z_recv,
    ag_send,
    ag_recv,
    n_send,
    n_recv,
    r_send,
    r_recv,
    in_sem,
    out_sem,
    kv_ss,
    kv_rs,
    q_ss,
    q_rs,
    d_ss,
    d_rs,
    w_ss,
    w_rs,
    f_ss,
    f_rs,
    n_ss,
    n_rs,
    r_ss,
    r_rs,
    below,
    above,
):
    nz, ny, nh = dims
    z = lax.axis_index("seq_0")
    y = lax.axis_index("seq_1")
    hd = lax.axis_index("head")
    s = z * ny + y
    shard_count = nz * ny

    def y_peer(d):
        return (z, lax.rem(y + d, ny), hd)

    def z_peer(d):
        return (lax.rem(z + d + nz, nz), y, hd)

    def h_peer(d):
        return (z, y, lax.rem(hd + d, nh))

    def s_peer(d):
        to = lax.rem(s + d + shard_count, shard_count)
        return (lax.div(to, ny), lax.rem(to, ny), hd)

    def remote(src, dst, ss, rs, to):
        return pltpu.make_async_remote_copy(
            src_ref=src, dst_ref=dst, send_sem=ss, recv_sem=rs, device_id=to, device_id_type=MESH
        )

    sent = []

    def on(condition, action):
        if condition is None:
            action()
        else:
            pl.when(condition)(action)

    def go(copy, condition=None):
        on(condition, copy.start)
        sent.append((copy, condition))
        return copy

    results = (
        (out, out_to),
        (dq_out, dq_to),
        (dk_out, dk_to),
        (dv_out, dv_to),
        (table_out, table_to),
        (gain_out, gain_to),
    )
    stores = []

    def store(n):
        stores.append(pltpu.make_async_copy(*results[n], out_sem.at[n]))
        stores[-1].start()

    barrier = pltpu.get_barrier_semaphore()
    last = shard_count - 1
    peers = [(s_peer(1), s < last), (s_peer(-1), s > 0)]
    if nz > 1:
        peers += [(z_peer(1), z < nz - 1), (z_peer(-1), z > 0)]
    peers += [(y_peer(d), None) for d in range(1, ny)]
    peers += [(h_peer(d), None) for d in range(1, nh)]

    def signal(sem, peer):
        pl.semaphore_signal(sem, inc=1, device_id=peer, device_id_type=MESH)

    expected = 0
    for peer, condition in peers:
        on(condition, functools.partial(signal, barrier, peer))
        expected = expected + (1 if condition is None else condition.astype(jnp.int32))

    loads = []
    targets = (own.at[0], own.at[1], own.at[2], own.at[3], table, index, window, gain)
    arrays = (k_in, v_in, q_in, g_in, table_in, index_in, window_in, gain_in)
    for n, (ref, target) in enumerate(zip(arrays, targets)):
        load = pltpu.make_async_copy(ref, target, in_sem.at[n])
        load.start()
        loads.append(load)
    loads[0].wait()
    loads[1].wait()
    K, V, Q, G = 0, 1, 2, 3

    for h in range(HEADS):
        state = tn(own[K, h], own[V, h])
        rs_send[0, :, h] = state.astype(BF).reshape(RING, PIECE, D)

    for j in range(1, REACH + 1):

        def clear_before(j=j):
            kv[j - 1] = jnp.zeros((2, HEADS, T, D), BF)

        def clear_after(j=j):
            qs[j - 1] = jnp.zeros((HEADS, T, D), BF)
            ds[j - 1] = jnp.zeros((HEADS, T, D), BF)
            if j < REACH:
                ws[j - 1] = jnp.zeros((16, T), F32)

        pl.when(s < j)(clear_before)
        pl.when(s + j > last)(clear_after)

    pl.semaphore_wait(barrier, expected)

    def scatter_start(side):
        copies = []
        for d in range(1, ny):
            to = lax.rem(y + d, ny)
            copies.append(
                go(
                    remote(
                        rs_send.at[side, to],
                        rs_recv.at[side, y],
                        f_ss.at[side, 0, d],
                        f_rs.at[side, 0, d],
                        y_peer(d),
                    )
                )
            )
        rs_recv[side, pl.ds(y, 1)] = rs_send[side, pl.ds(y, 1)]
        return copies

    def comes(side, d):
        return z >= d if side == 0 else z + d < nz

    def leaves(side, d):
        return z + d < nz if side == 0 else z >= d

    def across_start(side, scattered):
        for copy in scattered:
            copy.wait_recv()
        half = RING // 2
        pieces = [rs_recv[side, n].astype(F32) for n in range(RING)]
        low = functools.reduce(jnp.add, pieces[:half])
        upper = functools.reduce(jnp.add, pieces[half:])
        z_send[side] = (low + upper).astype(BF)
        copies = []
        for d in range(1, nz):
            copies.append(
                go(
                    remote(
                        z_send.at[side],
                        z_recv.at[side, d],
                        f_ss.at[side, 1, d],
                        f_rs.at[side, 1, d],
                        z_peer(d if side == 0 else -d),
                    ),
                    leaves(side, d),
                )
            )
        return copies, (low if side == 0 else upper)

    def gather_start(side, across, near):
        total = jnp.zeros((HEADS, PIECE, D), F32)
        for d in range(1, nz):
            counts = comes(side, d)
            on(counts, across[d - 1].wait_recv)
            other = lax.rem((z - d if side == 0 else z + d) + nz, nz)
            scale = jnp.where(
                lax.div(other, 2) == lax.div(z, 2),
                level_scale(T * 8),
                jnp.where(
                    lax.div(other, 4) == lax.div(z, 4), level_scale(T * 16), level_scale(T * 32)
                ),
            )
            total = total + jnp.where(counts, z_recv[side, d].astype(F32) * scale, 0.0)
        with_near = (total + near * level_scale(T * 4)).astype(BF)
        plain = total.astype(BF)
        ag_send[side, 0] = plain if side == 0 else with_near
        ag_send[side, 1] = with_near if side == 0 else plain
        copies = []
        for d in range(1, ny):
            to = lax.rem(y + d, ny)
            copies.append(
                go(
                    remote(
                        ag_send.at[side, lax.div(to, RING // 2)],
                        ag_recv.at[side, y],
                        f_ss.at[side, 2, d],
                        f_rs.at[side, 2, d],
                        y_peer(d),
                    )
                )
            )
        ag_recv[side, pl.ds(y, 1)] = ag_send[side, pl.ds(lax.div(y, RING // 2), 1)]
        return copies

    def gathered(side, h):
        return ag_recv[side, :, h].reshape(D, D)

    def before(j):
        return s >= j

    def after(j):
        return s + j <= last

    def forward(src, dst, ss, rs, j):
        return go(remote(src, dst, ss, rs, s_peer(1)), (s >= j - 1) & (s < last))

    def backward(src, dst, ss, rs, j):
        return go(remote(src, dst, ss, rs, s_peer(-1)), (s + j - 1 <= last) & (s > 0))

    def kv_hop(j, c):
        src = (k_in, v_in)[c] if j == 1 else kv.at[j - 2, c]
        return forward(src, kv.at[j - 1, c], kv_ss.at[j - 1, c], kv_rs.at[j - 1, c], j)

    def q_hop(j):
        src = q_in if j == 1 else qs.at[j - 2]
        return backward(src, qs.at[j - 1], q_ss.at[j - 1], q_rs.at[j - 1], j)

    def w_hop(j):
        src = w_own if j == 1 else ws.at[j - 2]
        return backward(src, ws.at[j - 1], w_ss.at[j - 1], w_rs.at[j - 1], j)

    def d_hop(j, h):
        src = dm.at[h] if j == 1 else ds.at[j - 2, h]
        return backward(src, ds.at[j - 1, h], d_ss.at[j - 1, h], d_rs.at[j - 1, h], j)

    def kv_step(j, c):
        on(before(j), kv_now[c].wait_recv)
        if j < REACH:
            kv_now[c] = kv_hop(j + 1, c)

    def q_step(j):
        on(after(j), q_now[0].wait_recv)
        if j < REACH:
            q_now[0] = q_hop(j + 1)
            on(after(j), w_now[0].wait_recv)
        if j < REACH - 1:
            w_now[0] = w_hop(j + 1)

    scattered = scatter_start(0)
    kv_now = [kv_hop(1, K), kv_hop(1, V)]
    q_now = [q_hop(1)]

    for load in loads[2:]:
        load.wait()
    index_row = index[...]
    for h in range(HEADS):
        rows = []
        for j in range(LEVELS):
            picked = index_row[j : j + 1]
            row = jnp.zeros((1, T), F32)
            for k in range(ROWS):
                row = jnp.where(picked == k, table[j, h, k], row)
            rows.append(row)
        rows.append(jnp.zeros((8 - LEVELS, T), F32))
        w_own[8 * h : 8 * h + 8] = jnp.concatenate(rows, axis=0)
    w_now = [w_hop(1)]
    spread = []
    for h in range(HEADS):
        for j in range(LEVELS):
            spread.append((iota((16, D), 0) == 8 * h + j).astype(BF))
    w_wide[...] = pick_tn(w_own[...], jnp.concatenate(spread, axis=1))

    def weight(h, j):
        at = (h * LEVELS + j) * D
        return w_wide[:, at : at + D]

    def window_scale(h, lanes):
        return lax.rsqrt(jnp.full((1, lanes), D * window[h], jnp.int32).astype(F32))

    token = iota((T, T), 0)
    key = iota((T, T), 1)
    pair_gap = token - key
    token_block = token >> 6
    key_block = key >> 6
    causal = pair_gap >= 0
    same_leaf = token_block == key_block
    same_pair = (token_block >> 1) == (key_block >> 1)

    def twice(half):
        return jnp.concatenate([half, half], axis=1)

    for h in range(HEADS):
        raw = nt(own[Q, h], own[K, h])
        scale0 = twice(weight(h, 0) * level_scale(BLOCK))
        scale1 = twice(weight(h, 1) * level_scale(BLOCK))
        scale2 = twice(weight(h, 2) * level_scale(2 * BLOCK))
        scale = jnp.where(same_leaf, scale0, jnp.where(same_pair, scale1, scale2))
        scale = jnp.where(causal, scale + window_scale(h, T), 0.0)
        low = (raw * scale).astype(BF)
        p_raw[h] = raw
        a_mix[h] = scale
        p_low[h] = low
        mix[h] = nn(low, own[V, h])

    def reach_q(h, j):
        limit = jnp.where(s >= j, window[h] - T * j, -T * (REACH + 1))
        return pair_gap < limit

    def reach_k(h, j):
        limit = jnp.where(s + j < shard_count, window[h] - T * j, -T * (REACH + 1))
        return -pair_gap < limit

    def far_probs(j):
        for h in range(HEADS):
            score = nt(own[K, h], qs[j - 1, h])
            p_far[j - 2, h] = jnp.where(reach_k(h, j), score, 0.0).astype(BF)

    def far_weights(j):
        spread = []
        for h in range(HEADS):
            for n in (3, 4):
                spread.append((iota((16, D), 0) == 8 * h + n).astype(BF))
        w_far[j - 1] = pick_tn(ws[j - 1], jnp.concatenate(spread, axis=1))

    odd = lax.rem(s, 2)
    odd_f = odd.astype(F32)
    second_f = lax.rem(lax.div(s, 2), 2).astype(F32)
    any_before = (s >= 1).astype(F32)
    any_after = (s + 1 < shard_count).astype(F32)

    def near_scale(h, wide):
        return window_scale(h, D) * any_before + wide * (odd_f * level_scale(T))

    def window_prob(h, j):
        score = nt(own[Q, h], kv[j - 1, K, h])
        return jnp.where(reach_q(h, j), score, 0.0).astype(BF)

    def window_part(h, j):
        return nn(window_prob(h, j), kv[j - 1, V, h]) * window_scale(h, D)

    if nz > 1:
        on(z > 0, lambda: pl.semaphore_wait(below, 1))
        on(z < nz - 1, lambda: signal(below, z_peer(1)))
        for d in range(1, nz):
            on(z >= d, functools.partial(signal, above, z_peer(-d)))

    kv_step(1, K)
    q_step(1)
    kv_step(1, V)
    if nz > 1:
        on(z < nz - 1, lambda: pl.semaphore_wait(above, nz - 1 - z))
    across, near = across_start(0, scattered)
    for h in range(HEADS):
        state = tn(kv[0, K, h], kv[0, V, h]).astype(BF)
        s_near[0, h] = state
        mix[h] = mix[h] + near_scale(h, weight(h, 3)) * nn(own[Q, h], state)

    kv_step(2, K)
    q_step(2)
    far_weights(1)
    kv_step(2, V)
    gather = gather_start(0, across, near)
    for h in range(HEADS):
        mix[h] = mix[h] + window_part(h, 2)

    kv_step(3, K)
    q_step(3)
    far_weights(2)
    far_probs(2)
    kv_step(3, V)
    for h in range(HEADS):
        state = tn(kv[odd, K, h], kv[odd, V, h]) + tn(kv[odd + 1, K, h], kv[odd + 1, V, h])
        state = (state * (second_f * level_scale(2 * T))).astype(BF)
        s_near[1, h] = state
        mix[h] = mix[h] + window_part(h, 3) + weight(h, 4) * nn(own[Q, h], state)
    for copy in gather:
        copy.wait_recv()
    for h in range(HEADS):
        mix[h] = mix[h] + weight(h, 5) * nn(own[Q, h], gathered(0, h))

    kv_step(4, K)
    last_probs = [window_prob(h, 4) for h in range(HEADS)]
    kv_step(4, V)
    square = jnp.zeros((T, D), F32)
    cross = jnp.zeros((T, D), F32)
    for h in range(HEADS):
        mixed = mix[h] + nn(last_probs[h], kv[3, V, h]) * window_scale(h, D)
        mix[h] = mixed
        square = square + mixed * mixed
        cross = cross + own[G, h].astype(F32) * gain[h : h + 1] * mixed

    both = jnp.concatenate([square, cross], axis=1)
    pick = (iota((16, 2 * D), 0) == (iota((16, 2 * D), 1) >> 7)).astype(BF)
    n_send[...] = pick_nt(pick, both)[0:8]
    norms = []
    for d in range(1, nh):
        norms.append(go(remote(n_send, n_recv.at[hd], n_ss.at[d], n_rs.at[d], h_peer(d))))
    n_recv[pl.ds(hd, 1)] = n_send[...][None]
    for copy in norms:
        copy.wait_recv()
    sums = functools.reduce(jnp.add, [n_recv[n] for n in range(nh)])
    inv_row = lax.rsqrt(sums[0:1] * (1.0 / (HEADS * nh * D)) + EPS)
    back_row = inv_row * inv_row * inv_row * sums[1:2] * (1.0 / (HEADS * nh * D))
    both_rows = jnp.concatenate([inv_row, back_row, jnp.zeros((14, T), F32)], axis=0)
    wide = pick_tn(both_rows, pick)
    inv_rms = wide[:, :D]
    back = wide[:, D:]

    grads = []
    for h in range(HEADS):
        given = own[G, h].astype(F32)
        grad = given * gain[h : h + 1] * inv_rms - mix[h] * back
        dm[h] = grad.astype(BF)
        grads.append(grad)
    for h in range(HEADS):
        up = (weight(h, 5) * grads[h]).astype(BF)
        state = tn(own[Q, h], up)
        rs_send[1, :, h] = state.astype(BF).reshape(RING, PIECE, D)
    scattered = scatter_start(1)
    d_now = [d_hop(1, h) for h in range(HEADS)]

    gain_rows = []
    for h in range(HEADS):
        scaled = mix[h] * inv_rms
        gain_rows.append(jnp.sum(own[G, h].astype(F32) * scaled, axis=0, keepdims=True))

    lane_block = iota((8, T), 1) >> 6
    row_no = iota((8, T), 0)
    block_ones = (iota((16, T), 0) == (iota((16, T), 1) >> 6)).astype(BF)
    hot = jnp.concatenate(
        [(index_row[j : j + 1] == iota((ROWS, T), 0)).astype(BF) for j in range(LEVELS)], axis=0
    )
    dq = []
    dk = []
    dv = []
    score_grads = []
    for h in range(HEADS):
        grad = grads[h]
        low = dm[h]
        prob_grad = nt(low, own[V, h])
        product = jnp.where(causal, p_raw[h] * prob_grad, 0.0)
        score_grads.append((prob_grad * a_mix[h]).astype(BF))
        by_block = pick_nt(block_ones, product)[0:8]
        row0 = jnp.sum(jnp.where(row_no == lane_block, by_block, 0.0), axis=0, keepdims=True)
        row1 = jnp.sum(
            jnp.where((row_no == lane_block - 1) & ((lane_block & 1) == 1), by_block, 0.0),
            axis=0,
            keepdims=True,
        )
        row2 = jnp.sum(
            jnp.where((row_no < 2) & (lane_block >= 2), by_block, 0.0), axis=0, keepdims=True
        )
        areas = jnp.concatenate(
            [
                grad * nn(own[Q, h], s_near[0, h]) * (odd_f * level_scale(T)),
                grad * nn(own[Q, h], s_near[1, h]),
                grad * nn(own[Q, h], gathered(0, h)),
            ],
            axis=1,
        )
        pick3 = (iota((16, 3 * D), 0) == (iota((16, 3 * D), 1) >> 7)).astype(BF)
        far_rows = pick_nt(pick3, areas)
        weight_rows = jnp.concatenate(
            [
                row0 * level_scale(BLOCK),
                row1 * level_scale(BLOCK),
                row2 * level_scale(2 * BLOCK),
                far_rows[0:3],
                jnp.zeros((10, T), F32),
            ],
            axis=0,
        )
        high, rest = halves(weight_rows)
        by_level = (nt(high, hot) + nt(rest, hot))[0:8]
        part = jnp.zeros((8, ROWS), F32)
        for j in range(LEVELS):
            slab = by_level[:, ROWS * j : ROWS * (j + 1)]
            part = part + jnp.where(iota((8, ROWS), 0) == j, slab, 0.0)
        r_send[0, 8 * h : 8 * h + 8] = jnp.concatenate(
            [part, jnp.zeros((8, D - ROWS), F32)], axis=1
        )

    r_send[0, 16:24] = jnp.concatenate(gain_rows + [jnp.zeros((6, D), F32)], axis=0)

    def reduce_start(step):
        count, me, peer = ((ny, y, y_peer), (nz, z, z_peer))[step]
        copies = []
        for d in range(1, count):
            copies.append(
                go(
                    remote(
                        r_send.at[step],
                        r_recv.at[step, me],
                        r_ss.at[step, d],
                        r_rs.at[step, d],
                        peer(d),
                    )
                )
            )
        r_recv[step, pl.ds(me, 1)] = r_send[step][None]
        return copies

    def reduce_end(step, copies):
        for copy in copies:
            copy.wait_recv()
        count = (ny, nz)[step]
        return functools.reduce(jnp.add, [r_recv[step, n] for n in range(count)])

    reduced = reduce_start(0)
    across, near = across_start(1, scattered)

    for h in range(HEADS):
        grad = grads[h]
        out[h] = (mix[h] * inv_rms * gain[h : h + 1]).astype(BF)
        dk.append(tn(score_grads[h], own[Q, h]))
        dv.append(tn(p_low[h], dm[h]))
        up1 = (near_scale(h, weight(h, 3)) * grad).astype(BF)
        up4 = (weight(h, 4) * grad).astype(BF)
        up5 = (weight(h, 5) * grad).astype(BF)
        dq.append(
            nn(score_grads[h], own[K, h])
            + nt(up1, s_near[0, h])
            + nt(up4, s_near[1, h])
            + nt(up5, gathered(0, h))
        )

    def d_step(j):
        for h in range(HEADS):
            on(after(j), d_now[h].wait_recv)
            if j < REACH:
                d_now[h] = d_hop(j + 1, h)

    def from_far(j):
        for h in range(HEADS):
            scale = window_scale(h, D)
            grad = ds[j - 1, h]
            dv[h] = dv[h] + nn(p_far[j - 2, h], grad) * scale
            back_score = jnp.where(reach_k(h, j), nt(own[V, h], grad), 0.0).astype(BF)
            dk[h] = dk[h] + nn(back_score, qs[j - 1, h]) * scale

    def to_far(j):
        for h in range(HEADS):
            back_score = jnp.where(reach_q(h, j), nt(dm[h], kv[j - 1, V, h]), 0.0).astype(BF)
            dq[h] = dq[h] + nn(back_score, kv[j - 1, K, h]) * window_scale(h, D)

    def far_weight(j, h, n):
        at = (2 * h + n) * D
        return w_far[j - 1, :, at : at + D]

    store(0)
    d_step(1)
    far_weights(3)
    far_probs(3)
    even_f = 1.0 - odd_f
    states = []
    for h in range(HEADS):
        scale = window_scale(h, D) * any_after + far_weight(1, h, 0) * (even_f * level_scale(T))
        states.append(tn(qs[0, h], (scale * ds[0, h].astype(F32)).astype(BF)))
    to_far(2)

    r_send[1] = reduce_end(0, reduced)
    reduced = reduce_start(1)
    d_step(2)
    to_far(3)
    from_far(2)

    d_step(3)
    q_step(4)
    far_probs(4)
    to_far(4)
    for h in range(HEADS):
        dq_out[h] = dq[h].astype(BF)
    store(1)
    from_far(3)
    first_f = 1.0 - second_f
    for h in range(HEADS):
        for n in range(2):
            slot = 1 - odd + n
            at = (2 * h + 1) * D
            scale = w_far[slot, :, at : at + D] * (first_f * level_scale(2 * T))
            states[h] = states[h] + tn(
                qs[slot, h], (scale * ds[slot, h].astype(F32)).astype(BF)
            )

    gather = gather_start(1, across, near)
    d_step(4)
    from_far(4)
    for copy in gather:
        copy.wait_recv()
    for h in range(HEADS):
        state = (states[h] + gathered(1, h).astype(F32)).astype(BF)
        dk_out[h] = (dk[h] + nt(own[V, h], state)).astype(BF)
        dv_out[h] = (dv[h] + nn(own[K, h], state)).astype(BF)

    store(2)
    store(3)
    total = reduce_end(1, reduced)
    for h in range(HEADS):
        table_out[:, h] = total[8 * h : 8 * h + LEVELS, 0:ROWS]
    gain_out[...] = total[16 : 16 + HEADS]
    store(4)
    store(5)
    for copy, condition in sent:
        on(condition, copy.wait_send)
    for copy in stores:
        copy.wait()


def place_kernel(*refs):
    arrays, targets, rest, (in_sem, out_sem) = refs[:6], refs[6:12], refs[12:18], refs[18:]
    loads = [pltpu.make_async_copy(arrays[n], rest[n], in_sem.at[n]) for n in range(6)]
    stores = [pltpu.make_async_copy(rest[n], targets[n], out_sem.at[n]) for n in range(6)]
    for load in loads:
        load.start()
    for load, store in zip(loads, stores):
        load.wait()
        store.start()
    for store in stores:
        store.wait()


def shards(
    dims,
    query_rows,
    key_rows,
    value_rows,
    norm_gain,
    level_table,
    level_index,
    window_length,
    out_grad,
):
    big = jax.ShapeDtypeStruct((HEADS, T, D), BF)
    nz, ny, nh = dims
    far = pl.BlockSpec(memory_space=pl.ANY)
    dma = pltpu.SemaphoreType.DMA
    results = pl.pallas_call(
        functools.partial(kernel, dims),
        out_shape=(
            big,
            big,
            big,
            big,
            jax.ShapeDtypeStruct((LEVELS, HEADS, ROWS), F32),
            jax.ShapeDtypeStruct((HEADS, D), F32),
        ),
        in_specs=[far] * 8,
        out_specs=[far] * 6,
        scratch_shapes=[
            pltpu.VMEM((HEADS, T, D), BF),
            pltpu.VMEM((HEADS, T, D), BF),
            pltpu.VMEM((HEADS, T, D), BF),
            pltpu.VMEM((HEADS, T, D), BF),
            pltpu.VMEM((LEVELS, HEADS, ROWS), F32),
            pltpu.VMEM((HEADS, D), F32),
            pltpu.VMEM((HEADS, D), F32),
            pltpu.SMEM((LEVELS, HEADS, ROWS), F32),
            pltpu.VMEM((LEVELS, T), jnp.int32),
            pltpu.SMEM((HEADS,), jnp.int32),
            pltpu.VMEM((4, HEADS, T, D), BF),
            pltpu.VMEM((REACH, 2, HEADS, T, D), BF),
            pltpu.VMEM((REACH, HEADS, T, D), BF),
            pltpu.VMEM((REACH, HEADS, T, D), BF),
            pltpu.VMEM((3, 16, T), F32),
            pltpu.VMEM((16, T), F32),
            pltpu.VMEM((T, HEADS * LEVELS * D), F32),
            pltpu.VMEM((3, T, HEADS * 2 * D), F32),
            pltpu.VMEM((HEADS, T, T), F32),
            pltpu.VMEM((HEADS, T, T), F32),
            pltpu.VMEM((HEADS, T, T), BF),
            pltpu.VMEM((3, HEADS, T, T), BF),
            pltpu.VMEM((2, HEADS, D, D), BF),
            pltpu.VMEM((HEADS, T, D), F32),
            pltpu.VMEM((HEADS, T, D), BF),
            pltpu.VMEM((2, RING, HEADS, PIECE, D), BF),
            pltpu.VMEM((2, RING, HEADS, PIECE, D), BF),
            pltpu.VMEM((2, HEADS, PIECE, D), BF),
            pltpu.VMEM((2, nz, HEADS, PIECE, D), BF),
            pltpu.VMEM((2, 2, HEADS, PIECE, D), BF),
            pltpu.VMEM((2, RING, HEADS, PIECE, D), BF),
            pltpu.VMEM((8, T), F32),
            pltpu.VMEM((nh, 8, T), F32),
            pltpu.VMEM((2, 24, D), F32),
            pltpu.VMEM((2, RING, 24, D), F32),
            dma((8,)),
            dma((6,)),
            dma((REACH, 2)),
            dma((REACH, 2)),
            dma((REACH,)),
            dma((REACH,)),
            dma((REACH, HEADS)),
            dma((REACH, HEADS)),
            dma((3,)),
            dma((3,)),
            dma((2, 3, RING)),
            dma((2, 3, RING)),
            dma((RING,)),
            dma((RING,)),
            dma((2, RING)),
            dma((2, RING)),
            pltpu.SemaphoreType.REGULAR,
            pltpu.SemaphoreType.REGULAR,
        ],
        compiler_params=pltpu.CompilerParams(
            collective_id=0, has_side_effects=True, vmem_limit_bytes=56 * 1024 * 1024
        ),
    )(
        query_rows,
        key_rows,
        value_rows,
        out_grad,
        norm_gain,
        jnp.transpose(level_table, (2, 1, 0)),
        level_index.T,
        window_length,
    )
    layer, dq, dk, dv, table_grad, gain_grad = pl.pallas_call(
        place_kernel,
        out_shape=[jax.ShapeDtypeStruct(r.shape, r.dtype) for r in results],
        in_specs=[far] * 6,
        out_specs=[far] * 6,
        scratch_shapes=[pltpu.VMEM(r.shape, r.dtype) for r in results] + [dma((6,)), dma((6,))],
        compiler_params=pltpu.CompilerParams(vmem_limit_bytes=56 * 1024 * 1024),
    )(*results)
    return layer, dq, dk, dv, jnp.transpose(table_grad, (2, 1, 0)), gain_grad


def solution(mesh):
    heads = mesh.shape["head"]
    dims = (mesh.shape["seq"] // RING, RING, heads)
    torus = Mesh(mesh.devices.reshape(*dims), ("seq_0", "seq_1", "head"))
    seq = ("seq_0", "seq_1")
    rows = P("head", seq, None)
    return jax.shard_map(
        functools.partial(shards, dims),
        mesh=torus,
        in_specs=(
            rows,
            rows,
            rows,
            P("head", None),
            P(None, "head", None),
            P(seq, None),
            P("head"),
            rows,
        ),
        out_specs=(rows, rows, rows, rows, P(None, "head", None), P("head", None)),
        check_vma=False,
    )
```
